32 devices in a mesh: grp: 8 (over z, y), head: 4 (over x, core).
Axes of the slice: x: 2, y: 2, z: 4, core: 2. Of those that a mesh axis runs over, the one named last changes fastest.
Arguments:
- long_queries: bfloat16 [4096, 64, 128], P(('grp', 'head')), may hold values from -24 to 24
- long_pairs: bfloat16 [4096, 8, 256], P(('grp', 'head')), may hold values from -24 to 24
- short_queries: bfloat16 [4096, 64, 128], P(('grp', 'head')), may hold values from -24 to 24
- short_pairs: bfloat16 [4096, 8, 256], P(('grp', 'head')), may hold values from -24 to 24
- doc_lengths: int32 [8, 8], replicated, may hold values from 1 to 128, 512 in all within a row
- destinations: int32 [8, 8], replicated, may hold values from 0 to 7, each once within a row
Outputs:
- long_result: bfloat16 [4096, 8192], P(('grp', 'head'))
- short_placed: bfloat16 [8192, 8192], P('grp', 'head')
The draws below stay inside these ranges and needn't reach their ends.
Inputs may be any that keep to these rules, and one draw needn't show every extreme that they name: `doc_lengths`: each row sums to 512, and each row has a document of exactly 128 tokens. `destinations`: each row is a permutation, so every group receives exactly one short document from every group.
All inputs are finite; a program needn't handle non-finite values.
Results may differ from the reference program's by a relative error of at most 0.0047.
Values may be sent and summed in bfloat16 or wider, within the bound.
No kernel may reach another device: no remote copies, remote signals or barrier semaphores. Data moves between devices by JAX's collectives and lax.ppermute only.
A program may use at most 128 MiB of HBM per device.

```python
import math
import jax
import jax.numpy as jnp
import numpy as np
from jax import lax

H = 64
KVH = 8
DH = 128
GROUPS = 8
LONG = 512
SHORT = 512
MAXDOC = 128
LONG_ROWS = 4096
SHORT_ROWS = 4096


def pair_draw(key, row_count):
    key_query, key_pair = jax.random.split(key, 2)
    queries = jax.random.normal(key_query, (row_count, H, DH), jnp.float32)
    pair_rows = jax.random.normal(key_pair, (row_count, KVH, 2 * DH), jnp.float32)
    queries = jnp.clip(queries, -24.0, 24.0).astype(jnp.bfloat16)
    pair_rows = jnp.clip(pair_rows, -24.0, 24.0).astype(jnp.bfloat16)
    return (queries, pair_rows)


def draw_long_queries(key, part):
    return pair_draw(jax.random.fold_in(key, 101), LONG_ROWS)[0]


def draw_long_pairs(key, part):
    return pair_draw(jax.random.fold_in(key, 101), LONG_ROWS)[1]


def draw_short_queries(key, part):
    return pair_draw(jax.random.fold_in(key, 202), SHORT_ROWS)[0]


def draw_short_pairs(key, part):
    return pair_draw(jax.random.fold_in(key, 202), SHORT_ROWS)[1]


def profile(count, total, bound, skew):
    weights = [(1 << 20) // math.isqrt(rank ** skew) + 1 for rank in range(2, count + 1)]
    spare, counts = total - bound - (count - 1), [1] * (count - 1)
    while spare > 0:
        free = [i for i in range(count - 1) if counts[i] < bound]
        whole, budget = sum([weights[i] for i in free]), spare
        for i in free:
            addition = min(bound - counts[i], max(1, budget * weights[i] // whole), spare)
            counts[i] = counts[i] + addition
            spare = spare - addition
    return np.array([bound] + counts)


def ragged_sizes(key, count, total, limit, slope):
    if count == 2:
        one = jax.random.randint(key, (), max(1, total - limit), min(limit, total - 1) + 1)
        return jnp.stack([one, total - one])
    sizes = jnp.asarray(profile(count, total, limit, slope), jnp.int32)
    pairs = (count - 1) // 2
    donor, taker = sizes[1:1 + 2 * pairs:2], sizes[2:2 + 2 * pairs:2]
    slack = jnp.minimum(donor - 1, limit - taker)
    moved = jax.random.randint(jax.random.fold_in(key, 1), (pairs,), 0, 1 << 20) % (slack + 1)
    sizes = sizes.at[1:1 + 2 * pairs:2].set(donor - moved).at[2:2 + 2 * pairs:2].set(taker + moved)
    return sizes[jax.random.permutation(jax.random.fold_in(key, 2), count)]


def setup_inputs(seed: int = 0) -> dict:
    key_of = jax.random.split(jax.random.key(seed), 7)
    return {
        "long_queries": draw_long_queries(jax.random.fold_in(key_of[6], 71), 0),
        "long_pairs": draw_long_pairs(jax.random.fold_in(key_of[6], 71), 0),
        "short_queries": draw_short_queries(jax.random.fold_in(key_of[6], 71), 0),
        "short_pairs": draw_short_pairs(jax.random.fold_in(key_of[6], 71), 0),
        "doc_lengths": jax.vmap(lambda own: ragged_sizes(own, GROUPS, SHORT, MAXDOC, 2))(jax.random.split(key_of[4], GROUPS)).reshape((GROUPS, GROUPS)).astype(jnp.int32),
        "destinations": jax.vmap(lambda own: jax.random.permutation(own, GROUPS))(jax.random.split(key_of[5], GROUPS)).reshape((GROUPS, GROUPS)).astype(jnp.int32),
    }


def attend_rows(queries, pair_rows, allowed):
    row_count = queries.shape[0]
    pair_heads = pair_rows.shape[1]
    head_size = queries.shape[2]
    group_size = queries.shape[1] // pair_heads
    grouped = queries.astype(jnp.float32).reshape(row_count, pair_heads, group_size, head_size)
    key_part = pair_rows[:, :, :head_size].astype(jnp.float32)
    value_part = pair_rows[:, :, head_size:].astype(jnp.float32)
    score_scale = 1.0 / math.sqrt(head_size)
    scores = jnp.einsum('qhgd,khd->hgqk', grouped, key_part) * score_scale
    scores = jnp.where(allowed[None, None], scores, -1e+30)
    row_max = lax.optimization_barrier(jnp.max(scores, axis=-1, keepdims=True))
    raised = jnp.exp(scores - row_max)
    weights = (raised / lax.optimization_barrier(jnp.sum(raised, axis=-1, keepdims=True))).astype(jnp.bfloat16)
    head_mix = jnp.einsum('hgqk,khd->qhgd', weights.astype(jnp.float32), value_part)
    return head_mix.reshape(row_count, queries.shape[1], head_size)

def long_group(packed):
    queries, pair_rows = packed
    position = jnp.arange(queries.shape[0], dtype=jnp.int32)
    allowed = position[None, :] <= position[:, None]
    return attend_rows(queries, pair_rows, allowed).astype(jnp.bfloat16)

def doc_attend(queries, pair_rows, length):
    position = jnp.arange(queries.shape[0], dtype=jnp.int32)
    allowed = (position[None, :] <= position[:, None]) & (position[None, :] < length)
    head_mix = attend_rows(queries, pair_rows, allowed)
    valid_rows = (position < length)[:, None, None]
    return jnp.where(valid_rows, head_mix, 0.0).astype(jnp.bfloat16)

def short_group(packed):
    queries, pair_rows, lengths, targets = packed
    starts = jnp.cumsum(lengths) - lengths
    position = jnp.arange(MAXDOC, dtype=jnp.int32)
    valid_rows = position[None, :] < lengths[:, None]
    row_index = jnp.where(valid_rows, starts[:, None] + position[None, :], 0).astype(jnp.int32)
    doc_out = jax.vmap(doc_attend)(queries[row_index], pair_rows[row_index], lengths)
    inverse = jnp.argsort(targets).astype(jnp.int32)
    return doc_out[inverse]

def reference(long_queries, long_pairs, short_queries, short_pairs, doc_lengths, destinations):
    long_all = lax.map(long_group, (long_queries.reshape(GROUPS, LONG, H, DH), long_pairs.reshape(GROUPS, LONG, KVH, 2 * DH)))
    long_result = long_all.reshape(GROUPS * LONG, H * DH)
    placed = lax.map(short_group, (short_queries.reshape(GROUPS, SHORT, H, DH), short_pairs.reshape(GROUPS, SHORT, KVH, 2 * DH), doc_lengths, destinations))
    short_placed = jnp.swapaxes(placed, 0, 1).reshape(GROUPS * GROUPS * MAXDOC, H * DH)
    return (long_result, short_placed)
```

```python
import functools
import math

import jax
import jax.numpy as jnp
from jax import lax
from jax.experimental import pallas as pl
from jax.experimental.pallas import tpu as pltpu
from jax.sharding import PartitionSpec as P

LOG2_E = 1.4426950408889634
VMEM_LIMIT = 48 * 1024 * 1024


def softmax_mix(queries, keys, values_and_ones, allowed, scale):
    scores = lax.dot_general(queries, keys, (((1,), (1,)), ((), ())), preferred_element_type=jnp.float32)
    scores = jnp.where(allowed, scores, -1e30)
    row_max = jnp.max(scores, axis=-1, keepdims=True)
    raised = jnp.exp2((scores - row_max) * scale).astype(jnp.bfloat16)
    both = jnp.dot(raised, values_and_ones, preferred_element_type=jnp.float32)
    size = keys.shape[1]
    return both[:, :size] / both[:, size:]


def with_ones(values):
    return jnp.concatenate([values, jnp.ones_like(values)], axis=1)


def long_kernel(first_ref, q_ref, kv_ref, out_ref, *, scale):
    rows, key_rows = q_ref.shape[0], kv_ref.shape[0]
    size = kv_ref.shape[1] // 2
    position = first_ref[0] + lax.broadcasted_iota(jnp.int32, (rows, key_rows), 0)
    allowed = lax.broadcasted_iota(jnp.int32, (rows, key_rows), 1) <= position
    keys, values = kv_ref[:, :size], with_ones(kv_ref[:, size:])
    for h in range(q_ref.shape[1] // size):
        columns = slice(h * size, (h + 1) * size)
        mixed = softmax_mix(q_ref[:, columns], keys, values, allowed, scale)
        out_ref[:, columns] = mixed.astype(out_ref.dtype)


def long_attend(queries, pairs, first_row, size):
    rows, width = queries.shape
    key_rows, pair_width = pairs.shape
    kv_heads = pair_width // (2 * size)
    share = width // kv_heads
    scores = rows * key_rows * (width // size)
    return pl.pallas_call(
        functools.partial(long_kernel, scale=LOG2_E / math.sqrt(size)),
        out_shape=jax.ShapeDtypeStruct((rows, width), jnp.bfloat16),
        grid=(kv_heads,),
        in_specs=[
            pl.BlockSpec(memory_space=pltpu.SMEM),
            pl.BlockSpec((rows, share), lambda c: (0, c)),
            pl.BlockSpec((key_rows, 2 * size), lambda c: (0, c)),
        ],
        out_specs=pl.BlockSpec((rows, share), lambda c: (0, c)),
        compiler_params=pltpu.CompilerParams(vmem_limit_bytes=VMEM_LIMIT),
        cost_estimate=pl.CostEstimate(
            flops=4 * scores * size, bytes_accessed=4 * rows * width + 2 * key_rows * pair_width, transcendentals=scores
        ),
        name="long_attend",
    )(first_row, queries, pairs)


def short_kernel(place_ref, lengths_ref, targets_ref, *refs, blocks, scale, size):
    q_blocks, kv_blocks = refs[:blocks], refs[blocks : 2 * blocks]
    out_ref, q_ref, kv_ref, mixed_ref, start_ref, length_ref = refs[2 * blocks :]
    slots, span, width = out_ref.shape
    rows = q_ref.shape[0]
    block_rows = rows // blocks
    group, own = place_ref[0], place_ref[1]
    for k in range(blocks):
        at = pl.ds(pl.multiple_of((own ^ k) * block_rows, block_rows), block_rows)
        q_ref[at, :] = q_blocks[k][:, :width]
        kv_ref[at, :] = kv_blocks[k][:, kv_blocks[k].shape[1] - 2 * size :]
    row = lax.broadcasted_iota(jnp.int32, (rows, 1), 0)
    begin = jnp.zeros((rows, 1), jnp.int32)
    start = jnp.int32(0)
    for j in range(slots):
        slot, length = targets_ref[group, j], lengths_ref[group, j]
        start_ref[slot] = start
        length_ref[slot] = length
        begin = jnp.where(row >= start, start, begin)
        start = start + length
    for first in range(0, rows, span):
        low = max(0, first - span)
        here = slice(first, first + span)
        window = slice(low, first + span)
        key_rows = first + span - low
        key_row = low + lax.broadcasted_iota(jnp.int32, (span, key_rows), 1)
        allowed = (key_row >= begin[here]) & (key_row <= row[here])
        keys, values = kv_ref[window, :size], with_ones(kv_ref[window, size:])
        for h in range(width // size):
            columns = slice(h * size, (h + 1) * size)
            mixed = softmax_mix(q_ref[here, columns], keys, values, allowed, scale)
            mixed_ref[here, columns] = mixed.astype(mixed_ref.dtype)
    place = lax.broadcasted_iota(jnp.int32, (span, rows), 0)
    source = lax.broadcasted_iota(jnp.int32, (span, rows), 1)
    for d in range(slots):
        chosen = (source == place + start_ref[d]) & (place < length_ref[d])
        picked = jnp.dot(chosen.astype(jnp.bfloat16), mixed_ref[...], preferred_element_type=jnp.float32)
        out_ref[d] = picked.astype(out_ref.dtype)


def short_attend(place, lengths, targets, query_blocks, pair_blocks, width, span, size):
    blocks = len(query_blocks)
    rows = blocks * query_blocks[0].shape[0]
    slots = lengths.shape[0]
    scores = 2 * rows * span * (width // size)
    smem = pl.BlockSpec(memory_space=pltpu.SMEM)
    vmem = pl.BlockSpec(memory_space=pltpu.VMEM)
    return pl.pallas_call(
        functools.partial(short_kernel, blocks=blocks, scale=LOG2_E / math.sqrt(size), size=size),
        out_shape=jax.ShapeDtypeStruct((slots, span, width), jnp.bfloat16),
        in_specs=[smem, smem, smem] + [vmem] * (2 * blocks),
        out_specs=vmem,
        scratch_shapes=[
            pltpu.VMEM((rows, width), jnp.bfloat16),
            pltpu.VMEM((rows, 2 * size), jnp.bfloat16),
            pltpu.VMEM((rows, width), jnp.bfloat16),
            pltpu.SMEM((slots,), jnp.int32),
            pltpu.SMEM((slots,), jnp.int32),
        ],
        compiler_params=pltpu.CompilerParams(vmem_limit_bytes=VMEM_LIMIT),
        cost_estimate=pl.CostEstimate(
            flops=16 * scores * size + 2 * slots * span * rows * width,
            bytes_accessed=2 * (rows * (width + 2 * size) + slots * span * width),
            transcendentals=scores,
        ),
        name="short_attend",
    )(place, lengths, targets, *query_blocks, *pair_blocks)


def swap_blocks(parts, axis):
    count = lax.axis_size(axis)
    own = lax.axis_index(axis)
    got = [lax.dynamic_index_in_dim(parts, own, 0, keepdims=False)]
    for k in range(1, count):
        sent = lax.dynamic_index_in_dim(parts, own ^ k, 0, keepdims=False)
        got.append(lax.ppermute(sent, axis, [(i, i ^ k) for i in range(count)]))
    return got


CHUNKS = ((0, 0, 2), (0, 2, 8), (1, 0, 8))


def on_device(long_queries, long_pairs, short_queries, short_pairs, doc_lengths, destinations):
    local_rows, heads, size = short_queries.shape
    kv_heads = short_pairs.shape[1]
    head_count, group_count = lax.axis_size("head"), lax.axis_size("grp")
    place = jnp.stack([lax.axis_index("grp"), lax.axis_index("head")]).astype(jnp.int32)
    span = 2 * local_rows * head_count // group_count
    own_heads, own_kv, share = heads // head_count, kv_heads // head_count, heads // kv_heads
    split_queries = short_queries.reshape(local_rows, head_count, own_heads * size)
    split_pairs = short_pairs.reshape(local_rows, head_count, own_kv * 2 * size)

    placed = []
    pair_blocks = {}
    for c, low, high in CHUNKS:
        if c >= own_kv:
            continue
        part = split_queries[:, :, (c * share + low) * size : (c * share + high) * size]
        if c not in pair_blocks:
            part = jnp.concatenate([part, split_pairs[:, :, c * 2 * size : (c + 1) * 2 * size]], axis=2)
        blocks = swap_blocks(jnp.swapaxes(part, 0, 1), "head")
        pair_blocks.setdefault(c, blocks)
        slots = short_attend(
            place, doc_lengths, destinations, blocks, pair_blocks[c], (high - low) * size, span, size
        )
        placed.append(lax.all_to_all(slots, "grp", split_axis=0, concat_axis=0, tiled=True))
    short_placed = jnp.concatenate(placed, axis=2).reshape(group_count * span, own_heads * size)

    all_pairs = lax.all_gather(long_pairs.reshape(local_rows, -1), "head", axis=0, tiled=True)
    first_row = (lax.axis_index("head") * local_rows).astype(jnp.int32).reshape(1)
    long_result = long_attend(long_queries.reshape(local_rows, -1), all_pairs, first_row, size)
    return (long_result, short_placed)


def solution(mesh):
    rows = P(("grp", "head"), None, None)
    return jax.shard_map(
        on_device,
        mesh=mesh,
        in_specs=(rows, rows, rows, rows, P(), P()),
        out_specs=(P(("grp", "head"), None), P("grp", "head")),
        check_vma=False,
    )
```

```python
import functools
import math

import jax
import jax.numpy as jnp
from jax import lax
from jax.experimental import pallas as pl
from jax.experimental.pallas import tpu as pltpu
from jax.sharding import PartitionSpec as P

LOG2_E = 1.4426950408889634
VMEM_LIMIT = 24 * 1024 * 1024


def softmax_mix(queries, keys, values_and_ones, allowed, scale):
    scores = lax.dot_general(queries, keys, (((1,), (1,)), ((), ())), preferred_element_type=jnp.float32)
    scores = jnp.where(allowed, scores, -1e30)
    row_max = jnp.max(scores, axis=-1, keepdims=True)
    raised = jnp.exp2((scores - row_max) * scale).astype(jnp.bfloat16)
    both = jnp.dot(raised, values_and_ones, preferred_element_type=jnp.float32)
    size = keys.shape[1]
    return both[:, :size] / both[:, size:]


def with_ones(values):
    return jnp.concatenate([values, jnp.ones_like(values)], axis=1)


def split_heads(scratch_ref, block):
    tokens, heads, size = block.shape
    scratch_ref[...] = block.astype(jnp.float32).reshape(tokens * heads, size)


def long_kernel(own_ref, q_ref, *refs, order, scale):
    kv_refs, (out_ref, scratch_ref) = refs[:-2], refs[-2:]
    rows, heads, size = q_ref.shape
    kv_here = kv_refs[0].shape[0]
    share = heads // kv_here
    own = own_ref[0]
    split_heads(scratch_ref, q_ref[...])
    row = lax.broadcasted_iota(jnp.int32, (rows, rows), 0)
    column = lax.broadcasted_iota(jnp.int32, (rows, rows), 1)
    allowed = jnp.concatenate(
        [column + ((own ^ k) - own) * rows <= row for k in order], axis=1
    )
    for c in range(kv_here):
        keys = jnp.concatenate([ref[c, :, :size] for ref in kv_refs], axis=0)
        values = with_ones(jnp.concatenate([ref[c, :, size:] for ref in kv_refs], axis=0))
        for h in range(c * share, (c + 1) * share):
            queries = scratch_ref[pl.ds(h, rows, stride=heads), :].astype(jnp.bfloat16)
            mixed = softmax_mix(queries, keys, values, allowed, scale)
            out_ref[:, h * size : (h + 1) * size] = mixed.astype(out_ref.dtype)


def long_attend(own, queries, pair_blocks, order):
    rows, heads, size = queries.shape
    kv_heads = pair_blocks[0].shape[0]
    kv_here = 2
    here = heads * kv_here // kv_heads
    scores = rows * rows * len(pair_blocks) * heads
    return pl.pallas_call(
        functools.partial(long_kernel, order=order, scale=LOG2_E / math.sqrt(size)),
        out_shape=jax.ShapeDtypeStruct((rows, heads * size), jnp.bfloat16),
        grid=(kv_heads // kv_here,),
        in_specs=[
            pl.BlockSpec(memory_space=pltpu.SMEM),
            pl.BlockSpec((rows, here, size), lambda c: (0, c, 0)),
        ]
        + [pl.BlockSpec((kv_here, rows, 2 * size), lambda c: (c, 0, 0))] * len(pair_blocks),
        out_specs=pl.BlockSpec((rows, here * size), lambda c: (0, c)),
        scratch_shapes=[pltpu.VMEM((rows * here, size), jnp.float32)],
        compiler_params=pltpu.CompilerParams(vmem_limit_bytes=VMEM_LIMIT),
        cost_estimate=pl.CostEstimate(flops=0, bytes_accessed=0, transcendentals=0),
        name="long_attend",
    )(own, queries, *pair_blocks)


def long_part(long_queries, long_pairs):
    own = lax.axis_index("head").astype(jnp.int32).reshape(1)
    return long_attend(own, long_queries, *share_blocks(jnp.swapaxes(long_pairs, 0, 1), "head"))


def share_blocks(block, axis):
    count = lax.axis_size(axis)
    blocks, order = [block], [0]
    step = count // 2
    while step:
        pairs = [(i, i ^ step) for i in range(count)]
        blocks += [lax.ppermute(b, axis, pairs) for b in blocks]
        order += [k ^ step for k in order]
        step //= 2
    return blocks, order


HEAD_CHUNKS = ((0, 6), (6, 16))


def prepare_kernel(own_ref, q_ref, kv_ref, *refs, count, low, high, kv_low, kv_high):
    out_refs, (q_scratch, kv_scratch) = refs[:-2], refs[-2:]
    tokens, heads, size = q_ref.shape
    kv_heads = kv_ref.shape[1]
    here, kv_here = heads // count, kv_heads // count
    if kv_low < kv_high:
        for part in range(2):
            split_heads(kv_scratch.at[part], kv_ref[:, :, part * size : (part + 1) * size])
    for k, out_ref in enumerate(out_refs):
        to = own_ref[0] ^ k
        split_heads(q_scratch, q_ref[:, pl.ds(pl.multiple_of(to * here, here), here), :])
        at = 0
        for h in range(low, high):
            picked = q_scratch[pl.ds(h, tokens, stride=here), :]
            out_ref[:, at : at + size] = picked.astype(out_ref.dtype)
            at += size
        for c in range(kv_low, kv_high):
            for part in range(2):
                picked = kv_scratch[part, pl.ds(to * kv_here + c, tokens, stride=kv_heads), :]
                out_ref[:, at : at + size] = picked.astype(out_ref.dtype)
                at += size


def prepare(own, queries, pairs, count, low, high, kv_low, kv_high):
    tokens, heads, size = queries.shape
    kv_heads = pairs.shape[1]
    width = (high - low + 2 * (kv_high - kv_low)) * size
    vmem = pl.BlockSpec(memory_space=pltpu.VMEM)
    return pl.pallas_call(
        functools.partial(prepare_kernel, count=count, low=low, high=high, kv_low=kv_low, kv_high=kv_high),
        out_shape=[jax.ShapeDtypeStruct((tokens, width), jnp.bfloat16)] * count,
        in_specs=[pl.BlockSpec(memory_space=pltpu.SMEM), vmem, vmem],
        out_specs=[vmem] * count,
        scratch_shapes=[
            pltpu.VMEM((tokens * heads // count, size), jnp.float32),
            pltpu.VMEM((2, tokens * kv_heads, size), jnp.float32),
        ],
        compiler_params=pltpu.CompilerParams(vmem_limit_bytes=VMEM_LIMIT),
        cost_estimate=pl.CostEstimate(flops=0, bytes_accessed=0, transcendentals=0),
        name="prepare",
    )(own, queries, pairs)


def slots_kernel(place_ref, lengths_ref, targets_ref, *refs, blocks, parts, scale):
    sources, (out_ref, q_ref, kv_ref, mixed_ref, start_ref, length_ref) = refs[:-6], refs[-6:]
    slots, span, width = out_ref.shape
    rows = q_ref.shape[0]
    size = kv_ref.shape[2] // 2
    block_rows = rows // blocks
    group, own = place_ref[0], place_ref[1]
    for k in range(blocks):
        at = pl.ds(pl.multiple_of((own ^ k) * block_rows, block_rows), block_rows)
        q_ref[at, :] = sources[k][:, :width]
        for c, (home, column, _, _) in enumerate(parts):
            kv_ref[c, at, :] = sources[home * blocks + k][:, column : column + 2 * size]
    row = lax.broadcasted_iota(jnp.int32, (rows, 1), 0)
    begin = jnp.zeros((rows, 1), jnp.int32)
    start = jnp.int32(0)
    for j in range(slots):
        slot, length = targets_ref[group, j], lengths_ref[group, j]
        start_ref[slot] = start
        length_ref[slot] = length
        begin = jnp.where(row >= start, start, begin)
        start = start + length
    for first in range(0, rows, span):
        low = max(0, first - span)
        here = slice(first, first + span)
        window = slice(low, first + span)
        key_row = low + lax.broadcasted_iota(jnp.int32, (span, first + span - low), 1)
        allowed = (key_row >= begin[here]) & (key_row <= row[here])
        for c, (_, _, head_low, head_high) in enumerate(parts):
            keys, values = kv_ref[c, window, :size], with_ones(kv_ref[c, window, size:])
            for h in range(head_low, head_high):
                columns = slice(h * size, (h + 1) * size)
                mixed = softmax_mix(q_ref[here, columns], keys, values, allowed, scale)
                mixed_ref[here, columns] = mixed.astype(mixed_ref.dtype)
    place = lax.broadcasted_iota(jnp.int32, (span, rows), 0)
    source = lax.broadcasted_iota(jnp.int32, (span, rows), 1)
    for d in range(slots):
        chosen = (source == place + start_ref[d]) & (place < length_ref[d])
        picked = jnp.dot(chosen.astype(jnp.bfloat16), mixed_ref[...], preferred_element_type=jnp.float32)
        out_ref[d] = picked.astype(out_ref.dtype)


def slots_attend(place, lengths, targets, sources, parts, blocks, width, span, size):
    rows = blocks * sources[0].shape[0]
    slots = lengths.shape[0]
    smem = pl.BlockSpec(memory_space=pltpu.SMEM)
    vmem = pl.BlockSpec(memory_space=pltpu.VMEM)
    return pl.pallas_call(
        functools.partial(slots_kernel, blocks=blocks, parts=parts, scale=LOG2_E / math.sqrt(size)),
        out_shape=jax.ShapeDtypeStruct((slots, span, width), jnp.bfloat16),
        in_specs=[smem, smem, smem] + [vmem] * len(sources),
        out_specs=vmem,
        scratch_shapes=[
            pltpu.VMEM((rows, width), jnp.bfloat16),
            pltpu.VMEM((len(parts), rows, 2 * size), jnp.bfloat16),
            pltpu.VMEM((rows, width), jnp.bfloat16),
            pltpu.SMEM((slots,), jnp.int32),
            pltpu.SMEM((slots,), jnp.int32),
        ],
        compiler_params=pltpu.CompilerParams(vmem_limit_bytes=VMEM_LIMIT),
        cost_estimate=pl.CostEstimate(flops=0, bytes_accessed=0, transcendentals=0),
        name="slots_attend",
    )(place, lengths, targets, *sources)


def lay_kernel(*refs, lows):
    pieces, (out_ref, sems) = refs[: len(lows)], refs[-2:]
    copies = []
    for i, (ref, low) in enumerate(zip(pieces, lows)):
        to = out_ref.at[:, :, low : low + ref.shape[2]]
        copies.append(pltpu.make_async_copy(ref, to, sems.at[i]))
        copies[-1].start()
    for copy in copies:
        copy.wait()


def lay(pieces, lows, columns, whole=None):
    anywhere = pl.BlockSpec(memory_space=pl.ANY)
    operands = pieces + ([] if whole is None else [whole])
    slots, span, _ = pieces[0].shape
    return pl.pallas_call(
        functools.partial(lay_kernel, lows=lows),
        out_shape=jax.ShapeDtypeStruct((slots, span, columns), jnp.bfloat16),
        in_specs=[anywhere] * len(operands),
        out_specs=anywhere,
        input_output_aliases={} if whole is None else {len(operands) - 1: 0},
        scratch_shapes=[pltpu.SemaphoreType.DMA((len(pieces),))],
        compiler_params=pltpu.CompilerParams(vmem_limit_bytes=VMEM_LIMIT),
        cost_estimate=pl.CostEstimate(flops=0, bytes_accessed=0, transcendentals=0),
        name="lay",
    )(*operands)


def after(value, *earlier):
    return lax.optimization_barrier((value, earlier))[0]


def on_device(long_queries, long_pairs, short_queries, short_pairs, doc_lengths, destinations):
    local_rows, heads, size = short_queries.shape
    kv_heads = short_pairs.shape[1]
    head_count, group_count = lax.axis_size("head"), lax.axis_size("grp")
    own = lax.axis_index("head").astype(jnp.int32).reshape(1)
    place = jnp.stack([lax.axis_index("grp"), lax.axis_index("head")]).astype(jnp.int32)
    span = 2 * local_rows * head_count // group_count
    own_heads, own_kv, share = heads // head_count, kv_heads // head_count, heads // kv_heads
    columns = own_heads * size
    chunks = [(low * own_heads // 16, high * own_heads // 16) for low, high in HEAD_CHUNKS]

    sent, homes = [], {}
    for i, (low, high) in enumerate(chunks):
        new = [c for c in range(own_kv) if c not in homes and c * share < high and low < (c + 1) * share]
        for j, c in enumerate(new):
            homes[c] = (i, (high - low + 2 * j) * size)
        kv_low, kv_high = (new[0], new[-1] + 1) if new else (0, 0)
        sent.append(prepare(own, short_queries, short_pairs, head_count, low, high, kv_low, kv_high))

    def swap(blocks):
        moved = [blocks[0]]
        for k in range(1, head_count):
            moved.append(lax.ppermute(blocks[k], "head", [(i, i ^ k) for i in range(head_count)]))
        return moved

    pairs_by_head = jnp.swapaxes(long_pairs, 0, 1)
    got, slots, whole = [], [], None
    for i, (low, high) in enumerate(chunks):
        if i:
            sent[i] = after(sent[i], got[i - 1][1:])
        got.append(swap(sent[i]))
        if i == 0:
            got[0] = after(got[0], sent[1:], pairs_by_head)
        else:
            got[i] = after(got[i], slots[i - 1])
        touched = [c for c in range(own_kv) if c * share < high and low < (c + 1) * share]
        order = [i] + sorted({homes[c][0] for c in touched} - {i})
        parts = [
            (order.index(homes[c][0]), homes[c][1], max(low, c * share) - low, min(high, (c + 1) * share) - low)
            for c in touched
        ]
        sources = [block for j in order for block in got[j]]
        slots.append(
            slots_attend(
                place, doc_lengths, destinations, sources, parts, head_count, (high - low) * size, span, size
            )
        )
    pairs_by_head = after(pairs_by_head, got[-1])
    shared, order = share_blocks(pairs_by_head, "head")
    long_queries = after(long_queries, slots[-1])
    long_result = long_attend(own, long_queries, shared, order)
    for i, (low, high) in enumerate(chunks):
        moved = lax.all_to_all(slots[i], "grp", split_axis=0, concat_axis=0, tiled=True)
        if i == len(chunks) - 1:
            moved = after(moved, long_result)
        whole = lay([moved], [low * size], columns, whole)
    return long_result, whole.reshape(group_count * span, columns)


def solution(mesh):
    rows = P(("grp", "head"), None, None)
    return jax.shard_map(
        on_device,
        mesh=mesh,
        in_specs=(rows, rows, rows, rows, P(), P()),
        out_specs=(P(("grp", "head"), None), P("grp", "head")),
        check_vma=False,
    )
```

```python
import functools
import math

import jax
import jax.numpy as jnp
from jax import lax
from jax.experimental import pallas as pl
from jax.experimental.pallas import tpu as pltpu
from jax.sharding import PartitionSpec as P

LOG2_E = 1.4426950408889634
COST = 10**11
VMEM_LIMIT = 24 * 1024 * 1024


def softmax_mix(queries, keys, values_and_ones, allowed, scale):
    scores = lax.dot_general(queries, keys, (((1,), (1,)), ((), ())), preferred_element_type=jnp.float32)
    scores = jnp.where(allowed, scores, -1e30)
    row_max = jnp.max(scores, axis=-1, keepdims=True)
    raised = jnp.exp2((scores - row_max) * scale).astype(jnp.bfloat16)
    both = jnp.dot(raised, values_and_ones, preferred_element_type=jnp.float32)
    size = keys.shape[1]
    return both[:, :size] / both[:, size:]


def with_ones(values):
    return jnp.concatenate([values, jnp.ones_like(values)], axis=1)


def split_heads(scratch_ref, block):
    tokens, heads, size = block.shape
    scratch_ref[...] = block.astype(jnp.float32).reshape(tokens * heads, size)


def long_kernel(own_ref, q_ref, *refs, order, scale):
    kv_refs, (out_ref, scratch_ref) = refs[:-2], refs[-2:]
    rows, heads, size = q_ref.shape
    kv_here = kv_refs[0].shape[0]
    share = heads // kv_here
    own = own_ref[0]
    split_heads(scratch_ref, q_ref[...])
    row = lax.broadcasted_iota(jnp.int32, (rows, rows), 0)
    column = lax.broadcasted_iota(jnp.int32, (rows, rows), 1)
    allowed = jnp.concatenate(
        [column + ((own ^ k) - own) * rows <= row for k in order], axis=1
    )
    for c in range(kv_here):
        keys = jnp.concatenate([ref[c, :, :size] for ref in kv_refs], axis=0)
        values = with_ones(jnp.concatenate([ref[c, :, size:] for ref in kv_refs], axis=0))
        for h in range(c * share, (c + 1) * share):
            queries = scratch_ref[pl.ds(h, rows, stride=heads), :].astype(jnp.bfloat16)
            mixed = softmax_mix(queries, keys, values, allowed, scale)
            out_ref[:, h * size : (h + 1) * size] = mixed.astype(out_ref.dtype)


def long_attend(own, queries, pair_blocks, order):
    rows, heads, size = queries.shape
    kv_heads = pair_blocks[0].shape[0]
    kv_here = 2
    here = heads * kv_here // kv_heads
    scores = rows * rows * len(pair_blocks) * heads
    return pl.pallas_call(
        functools.partial(long_kernel, order=order, scale=LOG2_E / math.sqrt(size)),
        out_shape=jax.ShapeDtypeStruct((rows, heads * size), jnp.bfloat16),
        grid=(kv_heads // kv_here,),
        in_specs=[
            pl.BlockSpec(memory_space=pltpu.SMEM),
            pl.BlockSpec((rows, here, size), lambda c: (0, c, 0)),
        ]
        + [pl.BlockSpec((kv_here, rows, 2 * size), lambda c: (c, 0, 0))] * len(pair_blocks),
        out_specs=pl.BlockSpec((rows, here * size), lambda c: (0, c)),
        scratch_shapes=[pltpu.VMEM((rows * here, size), jnp.float32)],
        compiler_params=pltpu.CompilerParams(vmem_limit_bytes=VMEM_LIMIT),
        cost_estimate=pl.CostEstimate(flops=0, bytes_accessed=0, transcendentals=0),
        name="long_attend",
    )(own, queries, *pair_blocks)


def long_part(long_queries, long_pairs):
    own = lax.axis_index("head").astype(jnp.int32).reshape(1)
    return long_attend(own, long_queries, *share_blocks(jnp.swapaxes(long_pairs, 0, 1), "head"))


def share_blocks(block, axis):
    count = lax.axis_size(axis)
    blocks, order = [block], [0]
    step = count // 2
    while step:
        pairs = [(i, i ^ step) for i in range(count)]
        blocks += [lax.ppermute(b, axis, pairs) for b in blocks]
        order += [k ^ step for k in order]
        step //= 2
    return blocks, order


HEAD_CHUNKS = ((0, 4), (4, 16))


def prepare_kernel(own_ref, q_ref, kv_ref, *refs, count, low, high, kv_low, kv_high):
    out_refs, (q_scratch, kv_scratch) = refs[:-2], refs[-2:]
    tokens, heads, size = q_ref.shape
    kv_heads = kv_ref.shape[1]
    here, kv_here = heads // count, kv_heads // count
    if kv_low < kv_high:
        for part in range(2):
            split_heads(kv_scratch.at[part], kv_ref[:, :, part * size : (part + 1) * size])
    for k in range(count):
        if len(out_refs) == 1:
            to, out_ref = k, out_refs[0].at[k]
        else:
            to, out_ref = own_ref[0] ^ k, out_refs[k]
        split_heads(q_scratch, q_ref[:, pl.ds(to * here if len(out_refs) == 1 else pl.multiple_of(to * here, here), here), :])
        at = 0
        for h in range(low, high):
            picked = q_scratch[pl.ds(h, tokens, stride=here), :]
            out_ref[:, at : at + size] = picked.astype(out_ref.dtype)
            at += size
        for c in range(kv_low, kv_high):
            for part in range(2):
                picked = kv_scratch[part, pl.ds(to * kv_here + c, tokens, stride=kv_heads), :]
                out_ref[:, at : at + size] = picked.astype(out_ref.dtype)
                at += size


def prepare(own, queries, pairs, count, low, high, kv_low, kv_high, stacked):
    tokens, heads, size = queries.shape
    kv_heads = pairs.shape[1]
    width = (high - low + 2 * (kv_high - kv_low)) * size
    vmem = pl.BlockSpec(memory_space=pltpu.VMEM)
    return pl.pallas_call(
        functools.partial(prepare_kernel, count=count, low=low, high=high, kv_low=kv_low, kv_high=kv_high),
        out_shape=[jax.ShapeDtypeStruct((count, tokens, width), jnp.bfloat16)]
        if stacked
        else [jax.ShapeDtypeStruct((tokens, width), jnp.bfloat16)] * count,
        in_specs=[pl.BlockSpec(memory_space=pltpu.SMEM), vmem, vmem],
        out_specs=[vmem] if stacked else [vmem] * count,
        scratch_shapes=[
            pltpu.VMEM((tokens * heads // count, size), jnp.float32),
            pltpu.VMEM((2, tokens * kv_heads, size), jnp.float32),
        ],
        compiler_params=pltpu.CompilerParams(vmem_limit_bytes=VMEM_LIMIT),
        cost_estimate=pl.CostEstimate(flops=0, bytes_accessed=0, transcendentals=0),
        name="prepare",
    )(own, queries, pairs)


def slots_kernel(place_ref, lengths_ref, targets_ref, *refs, sets, outs, parts, scale):
    count = sum(sets)
    sources, out_refs = refs[:count], refs[count : count + outs]
    q_ref, kv_ref, mixed_ref, start_ref, length_ref = refs[count + outs :]
    slots = lengths_ref.shape[1]
    span, width = out_refs[0].shape[-2:]
    rows = q_ref.shape[0]
    size = kv_ref.shape[2] // 2
    group, own = place_ref[0], place_ref[1]
    firsts = [sum(sets[:i]) for i in range(len(sets))]

    def fill(to_ref, home, columns):
        if sets[home] == 1:
            ref = sources[firsts[home]]
            for m in range(ref.shape[0]):
                to_ref[m * ref.shape[1] : (m + 1) * ref.shape[1], :] = ref[m, :, columns]
        else:
            for k in range(sets[home]):
                ref = sources[firsts[home] + k]
                at = pl.ds(pl.multiple_of((own ^ k) * ref.shape[0], ref.shape[0]), ref.shape[0])
                to_ref[at, :] = ref[:, columns]

    fill(q_ref, 0, slice(0, width))
    for c, (home, column, _, _) in enumerate(parts):
        fill(kv_ref.at[c], home, slice(column, column + 2 * size))
    row = lax.broadcasted_iota(jnp.int32, (rows, 1), 0)
    begin = jnp.zeros((rows, 1), jnp.int32)
    start = jnp.int32(0)
    for j in range(slots):
        slot, length = targets_ref[group, j], lengths_ref[group, j]
        start_ref[slot] = start
        length_ref[slot] = length
        begin = jnp.where(row >= start, start, begin)
        start = start + length
    for first in range(0, rows, span):
        low = max(0, first - span)
        here = slice(first, first + span)
        window = slice(low, first + span)
        key_row = low + lax.broadcasted_iota(jnp.int32, (span, first + span - low), 1)
        allowed = (key_row >= begin[here]) & (key_row <= row[here])
        for c, (_, _, head_low, head_high) in enumerate(parts):
            keys, values = kv_ref[c, window, :size], with_ones(kv_ref[c, window, size:])
            for h in range(head_low, head_high):
                columns = slice(h * size, (h + 1) * size)
                mixed = softmax_mix(q_ref[here, columns], keys, values, allowed, scale)
                mixed_ref[here, columns] = mixed.astype(mixed_ref.dtype)
    place = lax.broadcasted_iota(jnp.int32, (span, rows), 0)
    source = lax.broadcasted_iota(jnp.int32, (span, rows), 1)
    for k in range(slots):
        d, out_ref = (k, out_refs[0].at[k]) if outs == 1 else (group ^ k, out_refs[k])
        chosen = (source == place + start_ref[d]) & (place < length_ref[d])
        picked = jnp.dot(chosen.astype(jnp.bfloat16), mixed_ref[...], preferred_element_type=jnp.float32)
        out_ref[...] = picked.astype(out_ref.dtype)


def slots_attend(place, lengths, targets, source_sets, parts, rows, width, span, size, split):
    slots = lengths.shape[0]
    smem = pl.BlockSpec(memory_space=pltpu.SMEM)
    vmem = pl.BlockSpec(memory_space=pltpu.VMEM)
    sets = tuple(len(blocks) for blocks in source_sets)
    sources = [block for blocks in source_sets for block in blocks]
    shape = (span, width) if split else (slots, span, width)
    outs = slots if split else 1
    return pl.pallas_call(
        functools.partial(
            slots_kernel, sets=sets, outs=outs, parts=parts, scale=LOG2_E / math.sqrt(size)
        ),
        out_shape=[jax.ShapeDtypeStruct(shape, jnp.bfloat16)] * outs,
        in_specs=[smem, smem, smem] + [vmem] * len(sources),
        out_specs=[vmem] * outs,
        scratch_shapes=[
            pltpu.VMEM((rows, width), jnp.bfloat16),
            pltpu.VMEM((len(parts), rows, 2 * size), jnp.bfloat16),
            pltpu.VMEM((rows, width), jnp.bfloat16),
            pltpu.SMEM((slots,), jnp.int32),
            pltpu.SMEM((slots,), jnp.int32),
        ],
        compiler_params=pltpu.CompilerParams(vmem_limit_bytes=VMEM_LIMIT),
        cost_estimate=pl.CostEstimate(flops=COST, bytes_accessed=0, transcendentals=0),
        name="slots_attend",
    )(place, lengths, targets, *sources)


def lay_kernel(place_ref, *refs, count, low):
    pieces, (out_ref, sems) = refs[:count], refs[-2:]
    width = pieces[0].shape[-1]
    copies = []
    for k, ref in enumerate(pieces):
        at = slice(low, low + width)
        to = out_ref.at[:, :, at] if count == 1 else out_ref.at[place_ref[0] ^ k, :, at]
        copies.append(pltpu.make_async_copy(ref, to, sems.at[k]))
        copies[-1].start()
    for copy in copies:
        copy.wait()


def lay(place, pieces, low, shape, whole=None):
    anywhere = pl.BlockSpec(memory_space=pl.ANY)
    operands = [place, *pieces] + ([] if whole is None else [whole])
    return pl.pallas_call(
        functools.partial(lay_kernel, count=len(pieces), low=low),
        out_shape=jax.ShapeDtypeStruct(shape, jnp.bfloat16),
        in_specs=[pl.BlockSpec(memory_space=pltpu.SMEM)] + [anywhere] * (len(operands) - 1),
        out_specs=anywhere,
        input_output_aliases={} if whole is None else {len(operands) - 1: 0},
        scratch_shapes=[pltpu.SemaphoreType.DMA((len(pieces),))],
        compiler_params=pltpu.CompilerParams(vmem_limit_bytes=VMEM_LIMIT),
        cost_estimate=pl.CostEstimate(flops=0, bytes_accessed=0, transcendentals=0),
        name="lay",
    )(*operands)


def after(value, *earlier):
    return lax.optimization_barrier((value, earlier))[0]


def on_device(long_queries, long_pairs, short_queries, short_pairs, doc_lengths, destinations):
    local_rows, heads, size = short_queries.shape
    kv_heads = short_pairs.shape[1]
    head_count, group_count = lax.axis_size("head"), lax.axis_size("grp")
    own = lax.axis_index("head").astype(jnp.int32).reshape(1)
    place = jnp.stack([lax.axis_index("grp"), lax.axis_index("head")]).astype(jnp.int32)
    span = 2 * local_rows * head_count // group_count
    own_heads, own_kv, share = heads // head_count, kv_heads // head_count, heads // kv_heads
    columns = own_heads * size
    chunks = [(low * own_heads // 16, high * own_heads // 16) for low, high in HEAD_CHUNKS]

    sent, homes = [], {}
    for i, (low, high) in enumerate(chunks):
        new = [c for c in range(own_kv) if c not in homes and c * share < high and low < (c + 1) * share]
        for j, c in enumerate(new):
            homes[c] = (i, (high - low + 2 * j) * size)
        kv_low, kv_high = (new[0], new[-1] + 1) if new else (0, 0)
        sent.append(
            prepare(own, short_queries, short_pairs, head_count, low, high, kv_low, kv_high, stacked=i > 0)
        )

    def swap(blocks, axis, count):
        return [blocks[0]] + [
            lax.ppermute(blocks[k], axis, [(i, i ^ k) for i in range(count)]) for k in range(1, count)
        ]

    pairs_by_head = jnp.swapaxes(long_pairs, 0, 1)
    got, slots = [], []
    split = [i == 0 and group_count <= 8 for i in range(len(chunks))]
    for i, (low, high) in enumerate(chunks):
        if i == 0:
            moved = swap(sent[0], "head", head_count)
            got.append([after(block, sent[1:], pairs_by_head) for block in moved])
        else:
            if i > 1:
                sent[i] = [after(sent[i][0], slots[i - 2])]
            moved = lax.all_to_all(sent[i][0], "head", split_axis=0, concat_axis=0, tiled=True)
            got.append([after(moved, slots[i - 1])])
        touched = [c for c in range(own_kv) if c * share < high and low < (c + 1) * share]
        order = [i] + sorted({homes[c][0] for c in touched} - {i})
        parts = [
            (order.index(homes[c][0]), homes[c][1], max(low, c * share) - low, min(high, (c + 1) * share) - low)
            for c in touched
        ]
        slots.append(
            slots_attend(
                place,
                doc_lengths,
                destinations,
                [got[j] for j in order],
                parts,
                head_count * local_rows,
                (high - low) * size,
                span,
                size,
                split[i],
            )
        )
    shared, order = share_blocks(after(pairs_by_head, got[-1]), "head")
    long_result = long_attend(own, after(long_queries, slots[-1]), shared, order)
    whole, far = None, None
    shape = (group_count, span, own_heads * size)
    for i, (low, high) in enumerate(chunks):
        if split[i]:
            near = [after(piece, slots[-1]) for piece in slots[i][: group_count // 2]]
            moved = swap([*near, *slots[i][group_count // 2 :]], "grp", group_count)
            far = moved[group_count // 2 :]
        else:
            moved = [lax.all_to_all(after(slots[i][0], far), "grp", split_axis=0, concat_axis=0, tiled=True)]
        if i == len(chunks) - 1:
            moved = [after(moved[0], long_result)]
        else:
            moved[0] = after(moved[0], long_result)
        whole = lay(place, moved, low * size, shape, whole)
    return long_result, whole.reshape(group_count * span, own_heads * size)


def solution(mesh):
    rows = P(("grp", "head"), None, None)
    return jax.shard_map(
        on_device,
        mesh=mesh,
        in_specs=(rows, rows, rows, rows, P(), P()),
        out_specs=(P(("grp", "head"), None), P("grp", "head")),
        check_vma=False,
    )
```

```python
import functools
import math

import jax
import jax.numpy as jnp
from jax import lax
from jax.experimental import pallas as pl
from jax.experimental.pallas import tpu as pltpu
from jax.sharding import PartitionSpec as P

LOG2_E = 1.4426950408889634
COST = 10**11
VMEM_LIMIT = 24 * 1024 * 1024


def softmax_mix(queries, keys, values_and_ones, allowed, scale):
    scores = lax.dot_general(queries, keys, (((1,), (1,)), ((), ())), preferred_element_type=jnp.float32)
    scores = jnp.where(allowed, scores, -1e30)
    row_max = jnp.max(scores, axis=-1, keepdims=True)
    raised = jnp.exp2((scores - row_max) * scale).astype(jnp.bfloat16)
    both = jnp.dot(raised, values_and_ones, preferred_element_type=jnp.float32)
    size = keys.shape[1]
    return both[:, :size] / both[:, size:]


def with_ones(values):
    return jnp.concatenate([values, jnp.ones_like(values)], axis=1)


def split_heads(scratch_ref, block):
    tokens, heads, size = block.shape
    scratch_ref[...] = block.astype(jnp.float32).reshape(tokens * heads, size)


def long_kernel(own_ref, q_ref, *refs, order, scale):
    kv_refs, (out_ref, scratch_ref) = refs[:-2], refs[-2:]
    rows, heads, size = q_ref.shape
    kv_here = kv_refs[0].shape[0]
    share = heads // kv_here
    own = own_ref[0]
    split_heads(scratch_ref, q_ref[...])
    row = lax.broadcasted_iota(jnp.int32, (rows, rows), 0)
    column = lax.broadcasted_iota(jnp.int32, (rows, rows), 1)
    allowed = jnp.concatenate(
        [column + ((own ^ k) - own) * rows <= row for k in order], axis=1
    )
    for c in range(kv_here):
        keys = jnp.concatenate([ref[c, :, :size] for ref in kv_refs], axis=0)
        values = with_ones(jnp.concatenate([ref[c, :, size:] for ref in kv_refs], axis=0))
        for h in range(c * share, (c + 1) * share):
            queries = scratch_ref[pl.ds(h, rows, stride=heads), :].astype(jnp.bfloat16)
            mixed = softmax_mix(queries, keys, values, allowed, scale)
            out_ref[:, h * size : (h + 1) * size] = mixed.astype(out_ref.dtype)


def long_attend(own, queries, pair_blocks, order):
    rows, heads, size = queries.shape
    kv_heads = pair_blocks[0].shape[0]
    kv_here = 2
    here = heads * kv_here // kv_heads
    scores = rows * rows * len(pair_blocks) * heads
    return pl.pallas_call(
        functools.partial(long_kernel, order=order, scale=LOG2_E / math.sqrt(size)),
        out_shape=jax.ShapeDtypeStruct((rows, heads * size), jnp.bfloat16),
        grid=(kv_heads // kv_here,),
        in_specs=[
            pl.BlockSpec(memory_space=pltpu.SMEM),
            pl.BlockSpec((rows, here, size), lambda c: (0, c, 0)),
        ]
        + [pl.BlockSpec((kv_here, rows, 2 * size), lambda c: (c, 0, 0))] * len(pair_blocks),
        out_specs=pl.BlockSpec((rows, here * size), lambda c: (0, c)),
        scratch_shapes=[pltpu.VMEM((rows * here, size), jnp.float32)],
        compiler_params=pltpu.CompilerParams(vmem_limit_bytes=VMEM_LIMIT),
        cost_estimate=pl.CostEstimate(flops=0, bytes_accessed=0, transcendentals=0),
        name="long_attend",
    )(own, queries, *pair_blocks)


def long_part(long_queries, long_pairs):
    own = lax.axis_index("head").astype(jnp.int32).reshape(1)
    return long_attend(own, long_queries, *share_blocks(jnp.swapaxes(long_pairs, 0, 1), "head"))


def share_blocks(block, axis):
    count = lax.axis_size(axis)
    blocks, order = [block], [0]
    step = count // 2
    while step:
        pairs = [(i, i ^ step) for i in range(count)]
        blocks += [lax.ppermute(b, axis, pairs) for b in blocks]
        order += [k ^ step for k in order]
        step //= 2
    return blocks, order


HEAD_CHUNKS = ((0, 4), (4, 8), (8, 16))


def prepare_kernel(own_ref, q_ref, kv_ref, *refs, count, low, high, kv_low, kv_high):
    out_refs, (q_in, kv_in, q_scratch, kv_scratch, sems) = refs[:-5], refs[-5:]
    _, tokens, here, size = q_in.shape
    kv_heads = kv_ref.shape[1]
    kv_here = kv_heads // count
    goes = [k if len(out_refs) == 1 else own_ref[0] ^ k for k in range(count)]
    copies = [pltpu.make_async_copy(kv_ref, kv_in, sems.at[count])]
    for k in range(count):
        heads = pl.ds(pl.multiple_of(goes[k] * here, here), here)
        copies.append(pltpu.make_async_copy(q_ref.at[:, heads, :], q_in.at[k], sems.at[k]))
    for copy in copies:
        copy.start()
    copies[0].wait()
    if kv_low < kv_high:
        for part in range(2):
            split_heads(kv_scratch.at[part], kv_in[:, :, part * size : (part + 1) * size])
    for k in range(count):
        out_ref = out_refs[0].at[k] if len(out_refs) == 1 else out_refs[k]
        copies[k + 1].wait()
        split_heads(q_scratch, q_in[k])
        at = 0
        for h in range(low, high):
            picked = q_scratch[pl.ds(h, tokens, stride=here), :]
            out_ref[:, at : at + size] = picked.astype(out_ref.dtype)
            at += size
        for c in range(kv_low, kv_high):
            for part in range(2):
                picked = kv_scratch[part, pl.ds(goes[k] * kv_here + c, tokens, stride=kv_heads), :]
                out_ref[:, at : at + size] = picked.astype(out_ref.dtype)
                at += size


def prepare(own, queries, pairs, count, low, high, kv_low, kv_high, stacked):
    tokens, heads, size = queries.shape
    kv_heads = pairs.shape[1]
    width = (high - low + 2 * (kv_high - kv_low)) * size
    vmem = pl.BlockSpec(memory_space=pltpu.VMEM)
    return pl.pallas_call(
        functools.partial(prepare_kernel, count=count, low=low, high=high, kv_low=kv_low, kv_high=kv_high),
        out_shape=[jax.ShapeDtypeStruct((count, tokens, width), jnp.bfloat16)]
        if stacked
        else [jax.ShapeDtypeStruct((tokens, width), jnp.bfloat16)] * count,
        in_specs=[pl.BlockSpec(memory_space=pltpu.SMEM), pl.BlockSpec(memory_space=pltpu.HBM), pl.BlockSpec(memory_space=pltpu.HBM)],
        out_specs=[vmem] if stacked else [vmem] * count,
        scratch_shapes=[
            pltpu.VMEM((count, tokens, heads // count, size), queries.dtype),
            pltpu.VMEM(pairs.shape, pairs.dtype),
            pltpu.VMEM((tokens * heads // count, size), jnp.float32),
            pltpu.VMEM((2, tokens * kv_heads, size), jnp.float32),
            pltpu.SemaphoreType.DMA((count + 1,)),
        ],
        compiler_params=pltpu.CompilerParams(vmem_limit_bytes=60 * 1024 * 1024),
        cost_estimate=pl.CostEstimate(flops=0, bytes_accessed=0, transcendentals=0),
        name="prepare",
    )(own, queries, pairs)


def slots_kernel(place_ref, lengths_ref, targets_ref, *refs, sets, outs, parts, skip, scale):
    count = sum(sets)
    sources, out_refs = refs[:count], refs[count : count + outs]
    q_ref, kv_ref, mixed_ref, start_ref, length_ref = refs[count + outs :]
    slots = lengths_ref.shape[1]
    span, width = out_refs[0].shape[-2:]
    rows = q_ref.shape[0]
    size = kv_ref.shape[2] // 2
    group, own = place_ref[0], place_ref[1]
    firsts = [sum(sets[:i]) for i in range(len(sets))]

    def fill(to_ref, home, columns):
        if sets[home] == 1:
            ref = sources[firsts[home]]
            for m in range(ref.shape[0]):
                to_ref[m * ref.shape[1] : (m + 1) * ref.shape[1], :] = ref[m, :, columns]
        else:
            for k in range(sets[home]):
                ref = sources[firsts[home] + k]
                at = pl.ds(pl.multiple_of((own ^ k) * ref.shape[0], ref.shape[0]), ref.shape[0])
                to_ref[at, :] = ref[:, columns]

    fill(q_ref, 0, slice(skip, skip + width))
    for c, (home, column, _, _) in enumerate(parts):
        fill(kv_ref.at[c], home, slice(column, column + 2 * size))
    row = lax.broadcasted_iota(jnp.int32, (rows, 1), 0)
    begin = jnp.zeros((rows, 1), jnp.int32)
    start = jnp.int32(0)
    for j in range(slots):
        slot, length = targets_ref[group, j], lengths_ref[group, j]
        start_ref[slot] = start
        length_ref[slot] = length
        begin = jnp.where(row >= start, start, begin)
        start = start + length
    for first in range(0, rows, span):
        low = max(0, first - span)
        here = slice(first, first + span)
        window = slice(low, first + span)
        key_row = low + lax.broadcasted_iota(jnp.int32, (span, first + span - low), 1)
        allowed = (key_row >= begin[here]) & (key_row <= row[here])
        for c, (_, _, head_low, head_high) in enumerate(parts):
            keys, values = kv_ref[c, window, :size], with_ones(kv_ref[c, window, size:])
            for h in range(head_low, head_high):
                columns = slice(h * size, (h + 1) * size)
                mixed = softmax_mix(q_ref[here, columns], keys, values, allowed, scale)
                mixed_ref[here, columns] = mixed.astype(mixed_ref.dtype)
    place = lax.broadcasted_iota(jnp.int32, (span, rows), 0)
    source = lax.broadcasted_iota(jnp.int32, (span, rows), 1)
    for k in range(slots):
        d, out_ref = (k, out_refs[0].at[k]) if outs == 1 else (group ^ k, out_refs[k])
        chosen = (source == place + start_ref[d]) & (place < length_ref[d])
        picked = jnp.dot(chosen.astype(jnp.bfloat16), mixed_ref[...], preferred_element_type=jnp.float32)
        out_ref[...] = picked.astype(out_ref.dtype)


def slots_attend(place, lengths, targets, source_sets, parts, skip, rows, width, span, size, split):
    slots = lengths.shape[0]
    smem = pl.BlockSpec(memory_space=pltpu.SMEM)
    vmem = pl.BlockSpec(memory_space=pltpu.VMEM)
    sets = tuple(len(blocks) for blocks in source_sets)
    sources = [block for blocks in source_sets for block in blocks]
    shape = (span, width) if split else (slots, span, width)
    outs = slots if split else 1
    return pl.pallas_call(
        functools.partial(
            slots_kernel, sets=sets, outs=outs, parts=parts, skip=skip * size, scale=LOG2_E / math.sqrt(size)
        ),
        out_shape=[jax.ShapeDtypeStruct(shape, jnp.bfloat16)] * outs,
        in_specs=[smem, smem, smem] + [vmem] * len(sources),
        out_specs=[vmem] * outs,
        scratch_shapes=[
            pltpu.VMEM((rows, width), jnp.bfloat16),
            pltpu.VMEM((len(parts), rows, 2 * size), jnp.bfloat16),
            pltpu.VMEM((rows, width), jnp.bfloat16),
            pltpu.SMEM((slots,), jnp.int32),
            pltpu.SMEM((slots,), jnp.int32),
        ],
        compiler_params=pltpu.CompilerParams(vmem_limit_bytes=VMEM_LIMIT),
        cost_estimate=pl.CostEstimate(flops=COST, bytes_accessed=0, transcendentals=0),
        name="slots_attend",
    )(place, lengths, targets, *sources)


def lay_kernel(place_ref, *refs, plan):
    pieces, (out_ref, sems) = refs[: len(plan)], refs[-2:]
    copies = []
    for ref, (k, runs) in zip(pieces, plan):
        for column, low, width in runs:
            from_ref = ref.at[..., column : column + width]
            to = out_ref.at[:, :, low : low + width]
            if k is not None:
                to = out_ref.at[place_ref[0] ^ k, :, low : low + width]
            copies.append(pltpu.make_async_copy(from_ref, to, sems.at[len(copies)]))
            copies[-1].start()
    for copy in copies:
        copy.wait()


def lay(place, pieces, plan, shape):
    anywhere = pl.BlockSpec(memory_space=pl.ANY)
    return pl.pallas_call(
        functools.partial(lay_kernel, plan=plan),
        out_shape=jax.ShapeDtypeStruct(shape, jnp.bfloat16),
        in_specs=[pl.BlockSpec(memory_space=pltpu.SMEM)] + [anywhere] * len(pieces),
        out_specs=anywhere,
        scratch_shapes=[pltpu.SemaphoreType.DMA((sum(len(runs) for _, runs in plan),))],
        compiler_params=pltpu.CompilerParams(vmem_limit_bytes=VMEM_LIMIT),
        cost_estimate=pl.CostEstimate(flops=0, bytes_accessed=0, transcendentals=0),
        name="lay",
    )(place, *pieces)


def after(value, *earlier):
    return lax.optimization_barrier((value, earlier))[0]


def on_device(long_queries, long_pairs, short_queries, short_pairs, doc_lengths, destinations):
    local_rows, heads, size = short_queries.shape
    kv_heads = short_pairs.shape[1]
    head_count, group_count = lax.axis_size("head"), lax.axis_size("grp")
    own = lax.axis_index("head").astype(jnp.int32).reshape(1)
    place = jnp.stack([lax.axis_index("grp"), lax.axis_index("head")]).astype(jnp.int32)
    span = 2 * local_rows * head_count // group_count
    own_heads, own_kv, share = heads // head_count, kv_heads // head_count, heads // kv_heads
    columns = own_heads * size
    chunks = [(low * own_heads // 16, high * own_heads // 16) for low, high in HEAD_CHUNKS]

    travels = [chunks[0], (chunks[1][0], chunks[-1][1])]
    sent, homes = [], {}
    for i, (low, high) in enumerate(travels):
        new = [c for c in range(own_kv) if c not in homes and c * share < high and low < (c + 1) * share]
        for j, c in enumerate(new):
            homes[c] = (i, (high - low + 2 * j) * size)
        kv_low, kv_high = (new[0], new[-1] + 1) if new else (0, 0)
        sent.append(
            prepare(own, short_queries, short_pairs, head_count, low, high, kv_low, kv_high, stacked=i == 1)
        )

    def hop(block, axis, k):
        return lax.ppermute(block, axis, [(i, i ^ k) for i in range(lax.axis_size(axis))])

    pairs_by_head = jnp.swapaxes(long_pairs, 0, 1)
    split = [i != 1 and group_count <= 8 for i in range(len(chunks))]
    half = group_count // 2
    first = [sent[0][0]] + [hop(sent[0][k], "head", k) for k in range(1, head_count)]
    rest = lax.all_to_all(sent[1][0], "head", split_axis=0, concat_axis=0, tiled=True)
    got = [[after(block, sent[1], pairs_by_head) for block in first], [rest]]
    slots, far = [], []
    for i, (low, high) in enumerate(chunks):
        part = min(i, 1)
        if i:
            got[1] = [after(got[1][0], slots[i - 1], *far[:1] if i == 2 else [])]
        touched = [c for c in range(own_kv) if c * share < high and low < (c + 1) * share]
        order = [part] + sorted({homes[c][0] for c in touched} - {part})
        parts = [
            (order.index(homes[c][0]), homes[c][1], max(low, c * share) - low, min(high, (c + 1) * share) - low)
            for c in touched
        ]
        slots.append(
            slots_attend(
                place,
                doc_lengths,
                destinations,
                [got[j] for j in order],
                parts,
                low - travels[part][0],
                head_count * local_rows,
                (high - low) * size,
                span,
                size,
                split[i],
            )
        )
        far.append([hop(slots[i][k], "grp", k) for k in range(half, group_count)] if split[i] else [])
    shared, order = share_blocks(after(pairs_by_head, slots[-1]), "head")
    long_result = long_attend(own, after(long_queries, slots[-1]), shared, order)
    pieces, plan = [], []
    for i in range(len(chunks)):
        low, width = chunks[i][0] * size, (chunks[i][1] - chunks[i][0]) * size
        if not split[i]:
            pieces.append(lax.all_to_all(slots[i][0], "grp", split_axis=0, concat_axis=0, tiled=True))
            plan.append((None, [(0, low, width)]))
            continue
        pieces += [slots[i][0], *far[i]]
        plan += [(k, [(0, low, width)]) for k in (0, *range(half, group_count))]
    if any(split):
        spread = [i for i in range(len(chunks)) if split[i]]
        runs, column = [], 0
        for i in spread:
            low, width = chunks[i][0] * size, (chunks[i][1] - chunks[i][0]) * size
            runs.append((column, low, width))
            column += width
        for k in range(1, half):
            both = jnp.concatenate([slots[i][k] for i in spread], axis=1)
            pieces.append(hop(both, "grp", k))
            plan.append((k, runs))
    pieces[0] = after(pieces[0], long_result)
    whole = lay(place, pieces, plan, (group_count, span, own_heads * size))
    return long_result, whole.reshape(group_count * span, own_heads * size)


def solution(mesh):
    rows = P(("grp", "head"), None, None)
    return jax.shard_map(
        on_device,
        mesh=mesh,
        in_specs=(rows, rows, rows, rows, P(), P()),
        out_specs=(P(("grp", "head"), None), P("grp", "head")),
        check_vma=False,
    )
```

```python
import functools
import math

import jax
import jax.numpy as jnp
from jax import lax
from jax.experimental import pallas as pl
from jax.experimental.pallas import tpu as pltpu
from jax.sharding import PartitionSpec as P

LOG2_E = 1.4426950408889634
COST = 10**11
VMEM_LIMIT = 24 * 1024 * 1024


def softmax_mix(queries, keys, values_and_ones, allowed, scale):
    scores = lax.dot_general(queries, keys, (((1,), (1,)), ((), ())), preferred_element_type=jnp.float32)
    scores = jnp.where(allowed, scores, -1e30)
    row_max = jnp.max(scores, axis=-1, keepdims=True)
    raised = jnp.exp2((scores - row_max) * scale).astype(jnp.bfloat16)
    both = jnp.dot(raised, values_and_ones, preferred_element_type=jnp.float32)
    size = keys.shape[1]
    return both[:, :size] / both[:, size:]


def with_ones(values):
    return jnp.concatenate([values, jnp.ones_like(values)], axis=1)


def split_heads(scratch_ref, block):
    tokens, heads, size = block.shape
    scratch_ref[...] = block.astype(jnp.float32).reshape(tokens * heads, size)


def long_kernel(own_ref, q_ref, *refs, order, scale):
    kv_refs, (out_ref, scratch_ref) = refs[:-2], refs[-2:]
    rows, heads, size = q_ref.shape
    kv_here = kv_refs[0].shape[0]
    share = heads // kv_here
    own = own_ref[0]
    split_heads(scratch_ref, q_ref[...])
    row = lax.broadcasted_iota(jnp.int32, (rows, rows), 0)
    column = lax.broadcasted_iota(jnp.int32, (rows, rows), 1)
    allowed = jnp.concatenate(
        [column + ((own ^ k) - own) * rows <= row for k in order], axis=1
    )
    for c in range(kv_here):
        keys = jnp.concatenate([ref[c, :, :size] for ref in kv_refs], axis=0)
        values = with_ones(jnp.concatenate([ref[c, :, size:] for ref in kv_refs], axis=0))
        for h in range(c * share, (c + 1) * share):
            queries = scratch_ref[pl.ds(h, rows, stride=heads), :].astype(jnp.bfloat16)
            mixed = softmax_mix(queries, keys, values, allowed, scale)
            out_ref[:, h * size : (h + 1) * size] = mixed.astype(out_ref.dtype)


def long_attend(own, queries, pair_blocks, order):
    rows, heads, size = queries.shape
    kv_heads = pair_blocks[0].shape[0]
    kv_here = 2
    here = heads * kv_here // kv_heads
    scores = rows * rows * len(pair_blocks) * heads
    return pl.pallas_call(
        functools.partial(long_kernel, order=order, scale=LOG2_E / math.sqrt(size)),
        out_shape=jax.ShapeDtypeStruct((rows, heads * size), jnp.bfloat16),
        grid=(kv_heads // kv_here,),
        in_specs=[
            pl.BlockSpec(memory_space=pltpu.SMEM),
            pl.BlockSpec((rows, here, size), lambda c: (0, c, 0)),
        ]
        + [pl.BlockSpec((kv_here, rows, 2 * size), lambda c: (c, 0, 0))] * len(pair_blocks),
        out_specs=pl.BlockSpec((rows, here * size), lambda c: (0, c)),
        scratch_shapes=[pltpu.VMEM((rows * here, size), jnp.float32)],
        compiler_params=pltpu.CompilerParams(vmem_limit_bytes=VMEM_LIMIT),
        cost_estimate=pl.CostEstimate(flops=0, bytes_accessed=0, transcendentals=0),
        name="long_attend",
    )(own, queries, *pair_blocks)


def long_part(long_queries, long_pairs):
    own = lax.axis_index("head").astype(jnp.int32).reshape(1)
    return long_attend(own, long_queries, *share_blocks(jnp.swapaxes(long_pairs, 0, 1), "head"))


def share_blocks(block, axis):
    count = lax.axis_size(axis)
    blocks, order = [block], [0]
    step = count // 2
    while step:
        pairs = [(i, i ^ step) for i in range(count)]
        blocks += [lax.ppermute(b, axis, pairs) for b in blocks]
        order += [k ^ step for k in order]
        step //= 2
    return blocks, order


HEAD_CHUNKS = ((0, 4), (4, 8), (8, 16))


def prepare_kernel(own_ref, q_ref, kv_ref, *refs, count, low, high, kv_low, kv_high):
    out_refs, (q_in, kv_in, q_scratch, kv_scratch, sems) = refs[:-5], refs[-5:]
    _, tokens, here, size = q_in.shape
    kv_heads = kv_ref.shape[1]
    kv_here = kv_heads // count
    tile_low, tile_high = low // 8 * 8, min(here, -(-high // 8) * 8)
    goes = [k if len(out_refs) == 1 else own_ref[0] ^ k for k in range(count)]
    copies = [pltpu.make_async_copy(kv_ref, kv_in, sems.at[count])]
    for k in range(count):
        heads = pl.ds(pl.multiple_of(goes[k] * here, here), here)
        copies.append(pltpu.make_async_copy(q_ref.at[:, heads, :], q_in.at[k], sems.at[k]))
    for copy in copies:
        copy.start()
    copies[0].wait()
    if kv_low < kv_high:
        for part in range(2):
            split_heads(kv_scratch.at[part], kv_in[:, :, part * size : (part + 1) * size])
    for k in range(count):
        out_ref = out_refs[0].at[k] if len(out_refs) == 1 else out_refs[k]
        copies[k + 1].wait()
        split_heads(q_scratch, q_in[k, :, tile_low:tile_high, :])
        at = 0
        for h in range(low, high):
            picked = q_scratch[pl.ds(h - tile_low, tokens, stride=tile_high - tile_low), :]
            out_ref[:, at : at + size] = picked.astype(out_ref.dtype)
            at += size
        for c in range(kv_low, kv_high):
            for part in range(2):
                picked = kv_scratch[part, pl.ds(goes[k] * kv_here + c, tokens, stride=kv_heads), :]
                out_ref[:, at : at + size] = picked.astype(out_ref.dtype)
                at += size


def prepare(own, queries, pairs, count, low, high, kv_low, kv_high, stacked):
    tokens, heads, size = queries.shape
    kv_heads = pairs.shape[1]
    width = (high - low + 2 * (kv_high - kv_low)) * size
    vmem = pl.BlockSpec(memory_space=pltpu.VMEM)
    return pl.pallas_call(
        functools.partial(prepare_kernel, count=count, low=low, high=high, kv_low=kv_low, kv_high=kv_high),
        out_shape=[jax.ShapeDtypeStruct((count, tokens, width), jnp.bfloat16)]
        if stacked
        else [jax.ShapeDtypeStruct((tokens, width), jnp.bfloat16)] * count,
        in_specs=[pl.BlockSpec(memory_space=pltpu.SMEM), pl.BlockSpec(memory_space=pltpu.HBM), pl.BlockSpec(memory_space=pltpu.HBM)],
        out_specs=[vmem] if stacked else [vmem] * count,
        scratch_shapes=[
            pltpu.VMEM((count, tokens, heads // count, size), queries.dtype),
            pltpu.VMEM(pairs.shape, pairs.dtype),
            pltpu.VMEM((tokens * (min(heads // count, -(-high // 8) * 8) - low // 8 * 8), size), jnp.float32),
            pltpu.VMEM((2, tokens * kv_heads, size), jnp.float32),
            pltpu.SemaphoreType.DMA((count + 1,)),
        ],
        compiler_params=pltpu.CompilerParams(vmem_limit_bytes=60 * 1024 * 1024),
        cost_estimate=pl.CostEstimate(flops=0, bytes_accessed=0, transcendentals=0),
        name="prepare",
    )(own, queries, pairs)


def slots_kernel(place_ref, lengths_ref, targets_ref, *refs, sets, outs, parts, skip, scale):
    count = sum(sets)
    sources, out_refs = refs[:count], refs[count : count + outs]
    q_ref, kv_ref, mixed_ref, start_ref, length_ref = refs[count + outs :]
    slots = lengths_ref.shape[1]
    span, width = out_refs[0].shape[-2:]
    rows = q_ref.shape[0]
    size = kv_ref.shape[2] // 2
    group, own = place_ref[0], place_ref[1]
    firsts = [sum(sets[:i]) for i in range(len(sets))]

    def fill(to_ref, home, columns):
        if sets[home] == 1:
            ref = sources[firsts[home]]
            for m in range(ref.shape[0]):
                to_ref[m * ref.shape[1] : (m + 1) * ref.shape[1], :] = ref[m, :, columns]
        else:
            for k in range(sets[home]):
                ref = sources[firsts[home] + k]
                at = pl.ds(pl.multiple_of((own ^ k) * ref.shape[0], ref.shape[0]), ref.shape[0])
                to_ref[at, :] = ref[:, columns]

    fill(q_ref, 0, slice(skip, skip + width))
    for c, (home, column, _, _) in enumerate(parts):
        fill(kv_ref.at[c], home, slice(column, column + 2 * size))
    row = lax.broadcasted_iota(jnp.int32, (rows, 1), 0)
    begin = jnp.zeros((rows, 1), jnp.int32)
    start = jnp.int32(0)
    for j in range(slots):
        slot, length = targets_ref[group, j], lengths_ref[group, j]
        start_ref[slot] = start
        length_ref[slot] = length
        begin = jnp.where(row >= start, start, begin)
        start = start + length
    for first in range(0, rows, span):
        low = max(0, first - span)
        here = slice(first, first + span)
        window = slice(low, first + span)
        key_row = low + lax.broadcasted_iota(jnp.int32, (span, first + span - low), 1)
        allowed = (key_row >= begin[here]) & (key_row <= row[here])
        for c, (_, _, head_low, head_high) in enumerate(parts):
            keys, values = kv_ref[c, window, :size], with_ones(kv_ref[c, window, size:])
            for h in range(head_low, head_high):
                columns = slice(h * size, (h + 1) * size)
                mixed = softmax_mix(q_ref[here, columns], keys, values, allowed, scale)
                mixed_ref[here, columns] = mixed.astype(mixed_ref.dtype)
    place = lax.broadcasted_iota(jnp.int32, (span, rows), 0)
    source = lax.broadcasted_iota(jnp.int32, (span, rows), 1)
    for k in range(slots):
        d, out_ref = (k, out_refs[0].at[k]) if outs == 1 else (group ^ k, out_refs[k])
        chosen = (source == place + start_ref[d]) & (place < length_ref[d])
        picked = jnp.dot(chosen.astype(jnp.bfloat16), mixed_ref[...], preferred_element_type=jnp.float32)
        out_ref[...] = picked.astype(out_ref.dtype)


def slots_attend(place, lengths, targets, source_sets, parts, skip, rows, width, span, size, split):
    slots = lengths.shape[0]
    smem = pl.BlockSpec(memory_space=pltpu.SMEM)
    vmem = pl.BlockSpec(memory_space=pltpu.VMEM)
    sets = tuple(len(blocks) for blocks in source_sets)
    sources = [block for blocks in source_sets for block in blocks]
    shape = (span, width) if split else (slots, span, width)
    outs = slots if split else 1
    return pl.pallas_call(
        functools.partial(
            slots_kernel, sets=sets, outs=outs, parts=parts, skip=skip * size, scale=LOG2_E / math.sqrt(size)
        ),
        out_shape=[jax.ShapeDtypeStruct(shape, jnp.bfloat16)] * outs,
        in_specs=[smem, smem, smem] + [vmem] * len(sources),
        out_specs=[vmem] * outs,
        scratch_shapes=[
            pltpu.VMEM((rows, width), jnp.bfloat16),
            pltpu.VMEM((len(parts), rows, 2 * size), jnp.bfloat16),
            pltpu.VMEM((rows, width), jnp.bfloat16),
            pltpu.SMEM((slots,), jnp.int32),
            pltpu.SMEM((slots,), jnp.int32),
        ],
        compiler_params=pltpu.CompilerParams(vmem_limit_bytes=VMEM_LIMIT),
        cost_estimate=pl.CostEstimate(flops=COST, bytes_accessed=0, transcendentals=0),
        name="slots_attend",
    )(place, lengths, targets, *sources)


def lay_kernel(place_ref, *refs, plan):
    pieces, (out_ref, sems) = refs[: len(plan)], refs[-2:]
    copies = []
    for ref, (k, runs) in zip(pieces, plan):
        for column, low, width in runs:
            from_ref = ref.at[..., column : column + width]
            to = out_ref.at[:, :, low : low + width]
            if k is not None:
                to = out_ref.at[place_ref[0] ^ k, :, low : low + width]
            copies.append(pltpu.make_async_copy(from_ref, to, sems.at[len(copies)]))
            copies[-1].start()
    for copy in copies:
        copy.wait()


def lay(place, pieces, plan, shape):
    anywhere = pl.BlockSpec(memory_space=pl.ANY)
    return pl.pallas_call(
        functools.partial(lay_kernel, plan=plan),
        out_shape=jax.ShapeDtypeStruct(shape, jnp.bfloat16),
        in_specs=[pl.BlockSpec(memory_space=pltpu.SMEM)] + [anywhere] * len(pieces),
        out_specs=anywhere,
        scratch_shapes=[pltpu.SemaphoreType.DMA((sum(len(runs) for _, runs in plan),))],
        compiler_params=pltpu.CompilerParams(vmem_limit_bytes=VMEM_LIMIT),
        cost_estimate=pl.CostEstimate(flops=0, bytes_accessed=0, transcendentals=0),
        name="lay",
    )(place, *pieces)


def after(value, *earlier):
    return lax.optimization_barrier((value, earlier))[0]


def on_device(long_queries, long_pairs, short_queries, short_pairs, doc_lengths, destinations):
    local_rows, heads, size = short_queries.shape
    kv_heads = short_pairs.shape[1]
    head_count, group_count = lax.axis_size("head"), lax.axis_size("grp")
    own = lax.axis_index("head").astype(jnp.int32).reshape(1)
    place = jnp.stack([lax.axis_index("grp"), lax.axis_index("head")]).astype(jnp.int32)
    span = 2 * local_rows * head_count // group_count
    own_heads, own_kv, share = heads // head_count, kv_heads // head_count, heads // kv_heads
    columns = own_heads * size
    chunks = [(low * own_heads // 16, high * own_heads // 16) for low, high in HEAD_CHUNKS]

    travels = [chunks[0], (chunks[1][0], chunks[-1][1])]
    sent, homes = [], {}
    for i, (low, high) in enumerate(travels):
        new = [c for c in range(own_kv) if c not in homes and c * share < high and low < (c + 1) * share]
        for j, c in enumerate(new):
            homes[c] = (i, (high - low + 2 * j) * size)
        kv_low, kv_high = (new[0], new[-1] + 1) if new else (0, 0)
        sent.append(
            prepare(own, short_queries, short_pairs, head_count, low, high, kv_low, kv_high, stacked=i == 1)
        )

    def hop(block, axis, k):
        return lax.ppermute(block, axis, [(i, i ^ k) for i in range(lax.axis_size(axis))])

    pairs_by_head = jnp.swapaxes(long_pairs, 0, 1)
    split = [i != 1 and group_count <= 8 for i in range(len(chunks))]
    half = group_count // 2
    first = [sent[0][0]] + [hop(sent[0][k], "head", k) for k in range(1, head_count)]
    rest = lax.all_to_all(sent[1][0], "head", split_axis=0, concat_axis=0, tiled=True)
    got = [[after(block, sent[1], pairs_by_head) for block in first], [rest]]
    slots, far = [], []
    for i, (low, high) in enumerate(chunks):
        part = min(i, 1)
        if i:
            got[1] = [after(got[1][0], slots[i - 1], *far[:1] if i == 2 else [])]
        touched = [c for c in range(own_kv) if c * share < high and low < (c + 1) * share]
        order = [part] + sorted({homes[c][0] for c in touched} - {part})
        parts = [
            (order.index(homes[c][0]), homes[c][1], max(low, c * share) - low, min(high, (c + 1) * share) - low)
            for c in touched
        ]
        slots.append(
            slots_attend(
                place,
                doc_lengths,
                destinations,
                [got[j] for j in order],
                parts,
                low - travels[part][0],
                head_count * local_rows,
                (high - low) * size,
                span,
                size,
                split[i],
            )
        )
        far.append([hop(slots[i][k], "grp", k) for k in range(half, group_count)] if split[i] else [])
    shared, order = share_blocks(after(pairs_by_head, slots[-1]), "head")
    long_result = long_attend(own, after(long_queries, slots[-1]), shared, order)
    pieces, plan = [], []
    for i in range(len(chunks)):
        low, width = chunks[i][0] * size, (chunks[i][1] - chunks[i][0]) * size
        if not split[i]:
            pieces.append(lax.all_to_all(slots[i][0], "grp", split_axis=0, concat_axis=0, tiled=True))
            plan.append((None, [(0, low, width)]))
            continue
        pieces += [slots[i][0], *far[i]]
        plan += [(k, [(0, low, width)]) for k in (0, *range(half, group_count))]
    if any(split):
        spread = [i for i in range(len(chunks)) if split[i]]
        runs, column = [], 0
        for i in spread:
            low, width = chunks[i][0] * size, (chunks[i][1] - chunks[i][0]) * size
            runs.append((column, low, width))
            column += width
        for k in range(1, half):
            both = jnp.concatenate([slots[i][k] for i in spread], axis=1)
            pieces.append(hop(both, "grp", k))
            plan.append((k, runs))
    pieces[0] = after(pieces[0], long_result)
    whole = lay(place, pieces, plan, (group_count, span, own_heads * size))
    return long_result, whole.reshape(group_count * span, own_heads * size)


def solution(mesh):
    rows = P(("grp", "head"), None, None)
    return jax.shard_map(
        on_device,
        mesh=mesh,
        in_specs=(rows, rows, rows, rows, P(), P()),
        out_specs=(P(("grp", "head"), None), P("grp", "head")),
        check_vma=False,
    )
```
